32 devices in a mesh: dp: 8 (over y, x, core), tensor: 4 (over z).
Axes of the slice: x: 2, y: 2, z: 4, core: 2. Of those that a mesh axis runs over, the one named last changes fastest.
Arguments:
- query: bfloat16 [128, 4096], P('dp', 'tensor'), may hold values from -8000 to 8000
- incoming_key: bfloat16 [128, 2048], P('dp', 'tensor'), may hold values from -4.5 to 4.5
- new_value: bfloat16 [128, 2048], P('dp', 'tensor'), may hold values from -4.5 to 4.5
- key_cache: bfloat16 [128, 256, 2048], P('dp', None, 'tensor'), may hold values from -4.5 to 4.5
- value_cache: bfloat16 [128, 256, 2048], P('dp', None, 'tensor'), may hold values from -4.5 to 4.5
- cache_len: int32 [128], P('dp'), may hold values from 2 to 256
- out_weight: bfloat16 [4096, 4608], P('tensor'), may hold values from -0.09375 to 0.09375
- residual: bfloat16 [128, 4608], P('dp'), may hold values from -6 to 6
- post_gain: float32 [4608], replicated, may hold values from 0.5 to 1.5
- final_gain: float32 [4608], replicated, may hold values from 0.5 to 1.5
- vocab_weight: bfloat16 [131072, 4608], P(('dp', 'tensor')), may hold values from -113 to 113
- sampled: int32 [128], P('dp'), may hold values from 0 to 131071
- stop_flag: int32 [128], P('dp'), may hold values from 0 to 1, as said below
Outputs:
- new_residual: bfloat16 [128, 4608], P('dp', 'tensor')
- token_logprob: float32 [128], P('dp')
- insert_rank: int32 [128], P('dp')
- released_slot_total: int32 [], replicated
The draws below stay inside these ranges and needn't reach their ends.
Inputs may be any that keep to these rules, and one draw needn't show every extreme that they name: `stop_flag`: each aligned block of 16 slots holds 1 to 16 stops.
All inputs are finite; a program needn't handle non-finite values.
Results may differ from the reference program's by a relative error of at most 0.0038.
The reference program's roundings to bfloat16 on the way (of `weight`, `attn` and `hidden`) count: a program that leaves them out, or rounds other values in their place, can miss the bound.
Values may be sent and summed in bfloat16 or wider, within the bound.
A program may use at most 128 MiB of HBM per device.

```python
import jax
import jax.numpy as jnp
from jax import lax

D = 4608
HEADS = 32
KV_HEADS = 16
HEAD_DIM = 128
VOCAB = 131072
SLOT_DEV = 16
CACHE = 256
SLOTS = 128


def joint_cache(key):
    first, second, third = jax.random.split(jax.random.fold_in(key, 7), 3)
    cache = jax.random.truncated_normal(first, -4.5, 4.5, (SLOTS, CACHE, KV_HEADS * HEAD_DIM), jnp.float32)
    query = jax.random.truncated_normal(second, -4.5, 4.5, (SLOTS, HEADS * HEAD_DIM), jnp.float32)
    group = HEADS // KV_HEADS
    target = jnp.exp(jax.random.uniform(third, (SLOTS,), jnp.float32, jnp.log(110.0), jnp.log(420.0)))
    chosen = jnp.arange(SLOTS) % 8 == 3
    lead = cache[:, 0].reshape(SLOTS, KV_HEADS, HEAD_DIM)
    norms = jnp.sum(lead * lead, axis=-1)
    strength = target[:, None] * 12.0 / norms
    scaled = strength[:, :, None] * lead
    aligned = jnp.broadcast_to(scaled[:, :, None, :], (SLOTS, KV_HEADS, group, HEAD_DIM)).reshape(SLOTS, HEADS * HEAD_DIM)
    query = jnp.where(chosen[:, None], aligned, query)
    factor = 1.0 - 2.0 / (target[:, None] + 4.0)
    nearby = (lead * factor[:, :, None]).reshape(SLOTS, KV_HEADS * HEAD_DIM)
    cache = cache.at[:, 1].set(jnp.where(chosen[:, None], nearby, cache[:, 1]))
    return (cache, query)


def draw_key_cache(key, part):
    cache, query = joint_cache(key)
    return cache.astype(jnp.bfloat16)


def draw_query(key, part):
    cache, query = joint_cache(key)
    return jnp.clip(query, -8000.0, 8000.0).astype(jnp.bfloat16)


def draw_vocab_weight(key, part):
    first, second, third = jax.random.split(jax.random.fold_in(key, 11), 3)
    weight = 0.05 * jax.random.truncated_normal(first, -6.0, 6.0, (VOCAB, D), jnp.float32)
    strong = jax.random.randint(second, (VOCAB,), 0, 32) == 0
    level = jnp.exp(jax.random.uniform(third, (VOCAB,), jnp.float32, jnp.log(40.0), jnp.log(100.0)))
    factor = level / (0.05 * jnp.sqrt(jnp.float32(D)))
    weight = jnp.where(strong[:, None], weight * factor[:, None], weight)
    return jnp.clip(weight, -113.0, 113.0).astype(jnp.bfloat16)


def draw_stop_flag(key, part):
    first, second = jax.random.split(jax.random.fold_in(key, 13))
    blocks = SLOTS // SLOT_DEV
    index = jnp.arange(blocks, dtype=jnp.int32)
    rising = 1 + (SLOT_DEV - 1) * index // max(blocks - 1, 1)
    jitter = jax.random.randint(first, (blocks,), 0, 2)
    counts = jnp.maximum(rising - jitter, 1)
    block_keys = jax.random.split(second, blocks)
    orders = jax.vmap(lambda k: jax.random.permutation(k, SLOT_DEV))(block_keys)
    return (orders < counts[:, None]).astype(jnp.int32).reshape(SLOTS)


def place_ends(entries, own_key, low, largest):
    spot = [jax.random.randint(jax.random.fold_in(own_key, axis), (), 0, length) for axis, length in enumerate(entries.shape)]
    longest = entries.shape.index(max(entries.shape))
    next_to = spot[:longest] + [(spot[longest] + 1) % entries.shape[longest]] + spot[longest + 1:]
    return entries.at[tuple(spot)].set(low).at[tuple(next_to)].set(largest)


def steps_of(stream_key, dims, cuts, least, top_value):
    def one(position, blocks):
        steps = jax.random.uniform(jax.random.fold_in(jax.random.fold_in(stream_key, 6), position), (blocks,), jnp.float32, least / len(cuts), top_value / len(cuts))
        return jnp.repeat(jnp.exp(steps), dims[position] // blocks).reshape((-1,) + (1,) * (len(dims) - position - 1))

    gain = one(*cuts[0])
    for cut in cuts[1:]:
        gain = gain * one(*cut)
    return gain


def gaussian(rng, shape, spread, reach, cuts=(), kind=jnp.bfloat16):
    result = spread * jax.random.normal(rng, shape, jnp.float32)
    if cuts:
        result = result * steps_of(rng, shape, cuts, -0.22, 0.18)
    return jnp.clip(result, -reach, reach).astype(kind)


def setup_inputs(seed: int = 0) -> dict:
    seeds = jax.random.split(jax.random.key(seed), 14)
    query = draw_query(jax.random.fold_in(seeds[13], 71), 0)
    incoming_key = gaussian(seeds[1], (SLOTS, KV_HEADS * HEAD_DIM), 1.0, 4.5, ((0, 8), (1, 4)))
    new_value = gaussian(seeds[2], (SLOTS, KV_HEADS * HEAD_DIM), 1.0, 4.5, ((0, 8), (1, 4)))
    key_cache = draw_key_cache(jax.random.fold_in(seeds[13], 71), 0)
    value_cache = gaussian(seeds[4], (SLOTS, CACHE, KV_HEADS * HEAD_DIM), 1.0, 4.5, ((0, 8), (2, 4)))
    cache_len = place_ends(jax.random.randint(seeds[5], (SLOTS,), 2, CACHE + 1), jax.random.fold_in(seeds[5], 1), 2, CACHE).astype(jnp.int32)
    out_weight = gaussian(seeds[6], (HEADS * HEAD_DIM, D), (HEADS * HEAD_DIM) ** -0.5, 0.09375, ((0, 4),))
    residual = gaussian(seeds[7], (SLOTS, D), 1.0, 6.0, ((0, 8),))
    post_gain = jnp.clip(1.0 + 0.1 * jax.random.normal(seeds[8], (D,), jnp.float32), 0.5, 1.5)
    final_gain = jnp.clip(1.0 + 0.1 * jax.random.normal(seeds[9], (D,), jnp.float32), 0.5, 1.5)
    vocab_weight = draw_vocab_weight(jax.random.fold_in(seeds[13], 71), 0)
    sampled = place_ends(jax.random.randint(seeds[11], (SLOTS,), 0, VOCAB), jax.random.fold_in(seeds[11], 1), 0, VOCAB - 1).astype(jnp.int32)
    stop_flag = draw_stop_flag(jax.random.fold_in(seeds[13], 71), 0)
    return {"query": query, "incoming_key": incoming_key, "new_value": new_value, "key_cache": key_cache, "value_cache": value_cache, "cache_len": cache_len, "out_weight": out_weight, "residual": residual, "post_gain": post_gain, "final_gain": final_gain, "vocab_weight": vocab_weight, "sampled": sampled, "stop_flag": stop_flag}


def attend_slot(items):
    query, incoming_key, new_value, key_cache, value_cache, length = items
    group = HEADS // KV_HEADS
    query_vector = query.astype(jnp.float32).reshape(KV_HEADS, group, HEAD_DIM)
    keys = key_cache.astype(jnp.float32).reshape(CACHE, KV_HEADS, HEAD_DIM)
    values = value_cache.astype(jnp.float32).reshape(CACHE, KV_HEADS, HEAD_DIM)
    self_key = incoming_key.astype(jnp.float32).reshape(KV_HEADS, HEAD_DIM)
    own_value = new_value.astype(jnp.float32).reshape(KV_HEADS, HEAD_DIM)
    scores = jnp.einsum('kgd,ckd->kgc', query_vector, keys) / 12.0
    self_entry = jnp.einsum('kgd,kd->kg', query_vector, self_key) / 12.0
    valid = jnp.arange(CACHE, dtype=jnp.int32)[None, None, :] < length
    scores = jnp.where(valid, scores, -1e+30)
    top = jnp.maximum(lax.optimization_barrier(jnp.max(scores, axis=-1)), self_entry)
    expo = jnp.where(valid, jnp.exp(scores - top[..., None]), 0.0)
    own_exp = jnp.exp(self_entry - top)
    total = lax.optimization_barrier(jnp.sum(expo, axis=-1)) + own_exp
    weight = (expo / total[..., None]).astype(jnp.bfloat16).astype(jnp.float32)
    own_weight = (own_exp / total).astype(jnp.bfloat16).astype(jnp.float32)
    attn = jnp.einsum('kgc,ckd->kgd', weight, values) + own_weight[..., None] * own_value[:, None, :]
    return attn.reshape(HEADS * HEAD_DIM).astype(jnp.bfloat16)

def reference(query, incoming_key, new_value, key_cache, value_cache, cache_len, out_weight, residual, post_gain, final_gain, vocab_weight, sampled, stop_flag):
    attn = lax.map(attend_slot, (query, incoming_key, new_value, key_cache, value_cache, cache_len))
    proj = jnp.dot(attn, out_weight, preferred_element_type=jnp.float32)
    post = proj * lax.rsqrt(lax.optimization_barrier(jnp.mean(proj * proj, axis=1, keepdims=True)) + 1e-06) * post_gain
    new_residual = (residual.astype(jnp.float32) + post).astype(jnp.bfloat16)
    mixed = new_residual.astype(jnp.float32)
    hidden = (mixed * lax.rsqrt(lax.optimization_barrier(jnp.mean(mixed * mixed, axis=1, keepdims=True)) + 1e-06) * final_gain).astype(jnp.bfloat16)
    logits = lax.dot_general(hidden, vocab_weight, (((1,), (1,)), ((), ())), preferred_element_type=jnp.float32)
    top = lax.optimization_barrier(jnp.max(logits, axis=1))
    total = jnp.log(lax.optimization_barrier(jnp.sum(jnp.exp(logits - top[:, None]), axis=1))) + top
    picked = jnp.take_along_axis(logits, sampled[:, None].astype(jnp.int32), axis=1)[:, 0]
    token_logprob = picked - total
    freed = (stop_flag == 1).astype(jnp.int32)
    before = (jnp.cumsum(freed) - freed).astype(jnp.int32)
    insert_rank = jnp.where(freed == 1, before, -1).astype(jnp.int32)
    released_slot_total = jnp.sum(freed).astype(jnp.int32)
    return (new_residual, token_logprob, insert_rank, released_slot_total)
```

```python
import functools

import jax
import jax.numpy as jnp
from jax import lax
from jax.experimental import pallas as pl
from jax.experimental.pallas import tpu as pltpu
from jax.sharding import PartitionSpec as P

HEAD_DIM = 128
LANES = 128
MESH = pl.DeviceIdType.MESH
F32 = jnp.float32
BF16 = jnp.bfloat16
NT = (((1,), (1,)), ((), ()))


def chunk_count(model):
    for count in (3, 2):
        if model % (count * LANES) == 0:
            return count
    return 1


def kernel(
    dp_n,
    t_n,
    tiles,
    q_h,
    ik_h,
    nv_h,
    kc_h,
    vc_h,
    len_s,
    ow_h,
    res_h,
    pg_h,
    fg_h,
    w_h,
    samp_s,
    stop_s,
    nr_o,
    f_o,
    i_o,
    q,
    ik,
    nv,
    kc,
    vc,
    ow,
    res,
    pg,
    fg,
    w,
    attn,
    psend,
    precv,
    resf,
    zfold,
    zbuf,
    nrf,
    hbuf,
    acc,
    ibuf,
    dstat,
    zstat,
    lsem,
    wsem,
    ps,
    pr,
    zs,
    zr,
    hs,
    hr,
    isn,
    irc,
    ds,
    dr,
    es,
    er,
):
    d = lax.axis_index("dp")
    t = lax.axis_index("tensor")
    slot_dev, model = res.shape
    positions = kc.shape[1]
    heads = q.shape[1] // HEAD_DIM
    kv = ik.shape[1] // HEAD_DIM
    group = heads // kv
    rows = slot_dev // t_n
    chunks = hbuf.shape[0]
    width = model // chunks
    slots = dp_n * slot_dev
    fold = zbuf.shape[2]
    chips = dp_n // 2
    half = slot_dev // 2
    vloc = w.shape[0]
    tile = vloc // tiles

    def at_dp(peer):
        return {"dp": peer, "tensor": t}

    def at_t(peer):
        return {"dp": d, "tensor": peer}

    barrier = pltpu.get_barrier_semaphore()
    for k in range(1, dp_n):
        pl.semaphore_signal(
            barrier, inc=1, device_id=at_dp((d + k) % dp_n), device_id_type=MESH
        )
    for k in range(1, t_n):
        pl.semaphore_signal(
            barrier, inc=1, device_id=at_t((t + k) % t_n), device_id_type=MESH
        )

    def local(src, dst, i):
        copy = pltpu.make_async_copy(src, dst, lsem.at[i])
        copy.start()
        return copy

    def remote(src, dst, s, r, dev):
        return pltpu.make_async_remote_copy(
            src_ref=src, dst_ref=dst, send_sem=s, recv_sem=r, device_id=dev, device_id_type=MESH
        )

    first = pl.ds(0, half)
    second = pl.ds(half, half)
    c_q = local(q_h, q, 0)
    c_ik = local(ik_h, ik, 1)
    c_k = [local(kc_h.at[first], kc.at[first], 2)]
    c_nv = local(nv_h, nv, 3)
    c_v = [local(vc_h.at[first], vc.at[first], 4)]
    c_k.append(local(kc_h.at[second], kc.at[second], 5))
    c_v.append(local(vc_h.at[second], vc.at[second], 6))
    c_ow = local(ow_h, ow, 7)
    c_res = local(res_h, res, 8)
    c_pg = local(pg_h, pg, 9)
    c_fg = local(fg_h, fg, 10)
    w_copies = [
        pltpu.make_async_copy(
            w_h.at[pl.ds(i * tile, tile)], w.at[pl.ds(i * tile, tile)], wsem.at[i]
        )
        for i in range(tiles)
    ]
    pending = list(w_copies)

    def issue(count):
        for _ in range(min(count, len(pending))):
            pending.pop(0).start()

    lane = lax.broadcasted_iota(jnp.int32, (8, slots), 1)
    sub = lax.broadcasted_iota(jnp.int32, (8, slots), 0)
    info = jnp.zeros((8, slots), jnp.int32)
    for i in range(slot_dev):
        freed = jnp.where(stop_s[i] == 1, 1, 0)
        info = jnp.where(lane == d * slot_dev + i, jnp.where(sub == 0, samp_s[i], freed), info)
    ibuf[d] = info

    pl.semaphore_wait(barrier, dp_n - 1 + t_n - 1)
    sent = []
    i_copies = []
    for k in range(1, dp_n):
        copy = remote(
            ibuf.at[d], ibuf.at[d], isn.at[k - 1], irc.at[k - 1], at_dp((d + k) % dp_n)
        )
        copy.start()
        i_copies.append(copy)
    sent += i_copies

    head_mask = lax.broadcasted_iota(
        jnp.int32, (heads, heads * HEAD_DIM), 1
    ) // HEAD_DIM == lax.broadcasted_iota(jnp.int32, (heads, heads * HEAD_DIM), 0)
    pos = lax.broadcasted_iota(jnp.int32, (heads, positions), 1)
    c_q.wait()
    c_ik.wait()
    qf = q[...].astype(F32)
    ikf = ik[...].astype(F32)
    for part in range(2):
        numbers = range(part * half, part * half + half)
        c_k[part].wait()
        issue(1)
        scores = []
        for b in numbers:
            x = jnp.where(head_mask, jnp.broadcast_to(qf[b : b + 1, :], head_mask.shape), 0.0)
            blocks = []
            for g in range(kv):
                block = x[:, g * group * HEAD_DIM : (g * group + 1) * HEAD_DIM]
                for j in range(g * group + 1, (g + 1) * group):
                    block = block + x[:, j * HEAD_DIM : (j + 1) * HEAD_DIM]
                blocks.append(block)
            spread = jnp.concatenate(blocks, axis=1)
            score = lax.dot_general(
                spread.astype(BF16), kc[b], NT, preferred_element_type=F32
            ) / 12.0
            own = jnp.sum(spread * ikf[b : b + 1, :], axis=1, keepdims=True) / 12.0
            scores.append((score, own))
        weights = []
        for b, (score, own) in zip(numbers, scores):
            valid = pos < len_s[b]
            score = jnp.where(valid, score, -1e30)
            top = jnp.maximum(jnp.max(score, axis=1, keepdims=True), own)
            expo = jnp.where(valid, jnp.exp(score - top), 0.0)
            own_exp = jnp.exp(own - top)
            total = jnp.sum(expo, axis=1, keepdims=True) + own_exp
            weights.append(((expo / total).astype(BF16), (own_exp / total).astype(BF16).astype(F32)))
        if part == 0:
            c_nv.wait()
            nvf = nv[...].astype(F32)
        c_v[part].wait()
        issue(1)
        for b, (weight, own) in zip(numbers, weights):
            mix = jnp.dot(weight, vc[b], preferred_element_type=F32) + own * nvf[b : b + 1, :]
            for h in range(heads):
                g = h // group
                attn[b : b + 1, h * HEAD_DIM : (h + 1) * HEAD_DIM] = mix[
                    h : h + 1, g * HEAD_DIM : (g + 1) * HEAD_DIM
                ]

    issue(1)
    c_res.wait()
    res_all = res[...].astype(F32)
    for s in range(t_n):
        resf[s] = res_all[s * rows : (s + 1) * rows, :]
    attn_b = attn[...].astype(BF16)
    c_ow.wait()
    issue(len(pending))
    for c in range(chunks):
        cols = slice(c * width, (c + 1) * width)
        partial = jnp.dot(attn_b, ow[:, cols], preferred_element_type=F32)
        for s in range(t_n):
            psend[s, :, cols] = partial[s * rows : (s + 1) * rows, :]
    p_copies = []
    for k in range(1, t_n):
        peer = (t + k) % t_n
        copy = remote(psend.at[peer], precv.at[k - 1], ps.at[k - 1], pr.at[k - 1], at_t(peer))
        copy.start()
        p_copies.append(copy)
    sent += p_copies
    c_pg.wait()
    c_fg.wait()
    proj = psend[t]
    for k in range(1, t_n):
        p_copies[k - 1].wait_recv()
        proj = proj + precv[k - 1]
    post = proj * lax.rsqrt(jnp.mean(proj * proj, axis=1, keepdims=True) + 1e-06) * pg[...]
    mixed = (resf[t] + post).astype(BF16).astype(F32)
    if t_n * fold != model:
        zfold[...] = jnp.zeros_like(zfold)
    for s in range(t_n):
        size = min(fold, model - s * fold)
        if size > 0:
            zfold[s * rows : (s + 1) * rows, 0:size] = mixed[:, s * fold : s * fold + size]
    zbuf[t] = zfold[...].astype(BF16)
    z_copies = []
    for k in range(1, t_n):
        copy = remote(
            zbuf.at[t], zbuf.at[t], zs.at[k - 1], zr.at[k - 1], at_t((t + k) % t_n)
        )
        copy.start()
        z_copies.append(copy)
    sent += z_copies
    for copy in z_copies:
        copy.wait_recv()
    for s in range(t_n):
        piece = zbuf[s].astype(F32)
        for f in range(t_n):
            size = min(fold, model - f * fold)
            if size > 0:
                nrf[s * rows : (s + 1) * rows, f * fold : f * fold + size] = piece[
                    f * rows : (f + 1) * rows, 0:size
                ]
    mixed = nrf[...]
    nr_o[...] = mixed.astype(BF16)
    hidden = (
        mixed * lax.rsqrt(jnp.mean(mixed * mixed, axis=1, keepdims=True) + 1e-06) * fg[...]
    ).astype(BF16)

    sibling = d + 1 - 2 * (d % 2)
    direct = {}
    for c in range(chunks):
        hbuf[c, d] = hidden[:, c * width : (c + 1) * width]
        here = hbuf.at[c, d]
        for k in range(1, chips):
            direct[c, k] = remote(
                here, here, hs.at[c, k], hr.at[c, k], at_dp((d + 2 * k) % dp_n)
            )
            direct[c, k].start()
        direct[c, 0] = remote(here, here, hs.at[c, 0], hr.at[c, 0], at_dp(sibling))
        direct[c, 0].start()
    sent += list(direct.values())
    passed = {}

    def pass_on(c):
        for k in range(1, chips):
            direct[c, k].wait_recv()
            there = hbuf.at[c, (d + dp_n - 2 * k) % dp_n]
            j = chips - 1 + k
            passed[c, k] = remote(there, there, hs.at[c, j], hr.at[c, j], at_dp(sibling))
            passed[c, k].start()
            sent.append(passed[c, k])

    for copy in i_copies:
        copy.wait_recv()
    info = ibuf[0]
    for j in range(1, dp_n):
        info = info + ibuf[j]
    flags = info[1:2, :]
    order = lax.broadcasted_iota(jnp.int32, (slots, slots), 0) < lax.broadcasted_iota(
        jnp.int32, (slots, slots), 1
    )
    flags8 = jnp.broadcast_to(flags, (8, slots)).astype(F32)
    before = jnp.dot(
        flags8.astype(BF16),
        jnp.where(order, 1.0, 0.0).astype(BF16),
        preferred_element_type=F32,
    )
    rank = jnp.where(flags8 > 0.5, before, -1.0)
    count = jnp.sum(flags8, axis=1, keepdims=True)
    i_o[...] = jnp.where(sub == 0, rank, count).astype(jnp.int32)
    start = (d * t_n + t) * vloc
    local_ids = info[0:1, :] - start

    pass_on(0)
    top = None
    for c in range(chunks):
        direct[c, 0].wait_recv()
        for k in range(1, chips):
            passed[c, k].wait_recv()
        state = hbuf[c].reshape(slots, width)
        for i in range(tiles):
            if c == 0:
                w_copies[i].wait()
            if c + 1 < chunks and i == tiles // 2:
                pass_on(c + 1)
            part = lax.dot_general(
                w[i * tile : (i + 1) * tile, c * width : (c + 1) * width],
                state,
                NT,
                preferred_element_type=F32,
            )
            if c > 0:
                part = part + acc[i * tile : (i + 1) * tile, :]
            if c + 1 < chunks:
                acc[i * tile : (i + 1) * tile, :] = part
                continue
            index = lax.broadcasted_iota(jnp.int32, (tile, slots), 0) + i * tile
            hit = jnp.sum(jnp.where(index == local_ids, part, 0.0), axis=0, keepdims=True)
            peak = jnp.max(part, axis=0, keepdims=True)
            if top is None:
                top = peak
                total = jnp.sum(jnp.exp(part - top), axis=0, keepdims=True)
                picked = hit
            else:
                larger = jnp.maximum(top, peak)
                total = total * jnp.exp(top - larger) + jnp.sum(
                    jnp.exp(part - larger), axis=0, keepdims=True
                )
                top = larger
                picked = picked + hit

    def pack(top, total, picked):
        return jnp.where(sub == 0, top, jnp.where(sub == 1, total, picked))

    def merge(parts):
        top = parts[0][0:1, :]
        for part in parts[1:]:
            top = jnp.maximum(top, part[0:1, :])
        total = jnp.zeros_like(top)
        picked = jnp.zeros_like(top)
        for part in parts:
            total = total + part[1:2, :] * jnp.exp(part[0:1, :] - top)
            picked = picked + part[2:3, :]
        return top, total, picked

    dstat[d] = pack(top, total, picked)
    copies = []
    for k in range(1, dp_n):
        copy = remote(dstat.at[d], dstat.at[d], ds.at[k - 1], dr.at[k - 1], at_dp((d + k) % dp_n))
        copy.start()
        copies.append(copy)
    for copy in copies:
        copy.wait_recv()
    sent += copies
    zstat[t] = pack(*merge([dstat[j] for j in range(dp_n)]))
    copies = []
    for k in range(1, t_n):
        copy = remote(zstat.at[t], zstat.at[t], es.at[k - 1], er.at[k - 1], at_t((t + k) % t_n))
        copy.start()
        copies.append(copy)
    for copy in copies:
        copy.wait_recv()
    sent += copies
    top, total, picked = merge([zstat[j] for j in range(t_n)])
    f_o[...] = jnp.broadcast_to(picked - (jnp.log(total) + top), (8, slots))
    for copy in sent:
        copy.wait_send()


def on_device(
    dp_n,
    t_n,
    query,
    incoming_key,
    new_value,
    key_cache,
    value_cache,
    cache_len,
    out_weight,
    residual,
    post_gain,
    final_gain,
    vocab_weight,
    sampled,
    stop_flag,
):
    slot_dev, model = residual.shape
    slots = slot_dev * dp_n
    rows = slot_dev // t_n
    fold = -(-model // (t_n * LANES)) * LANES
    chunks = chunk_count(model)
    vloc = vocab_weight.shape[0]
    tiles = max(1, vloc // 512)
    dma = pltpu.SemaphoreType.DMA
    anywhere = pl.BlockSpec(memory_space=pl.ANY)
    smem = pl.BlockSpec(memory_space=pltpu.SMEM)
    vmem = pl.BlockSpec(memory_space=pltpu.VMEM)

    def like(a):
        return pltpu.VMEM(a.shape, a.dtype)

    pg = post_gain.reshape(1, model)
    fg = final_gain.reshape(1, model)
    mixed, logs, ranks = pl.pallas_call(
        functools.partial(kernel, dp_n, t_n, tiles),
        out_shape=(
            jax.ShapeDtypeStruct((slot_dev, model), BF16),
            jax.ShapeDtypeStruct((8, slots), F32),
            jax.ShapeDtypeStruct((8, slots), jnp.int32),
        ),
        in_specs=[anywhere] * 5 + [smem] + [anywhere] * 5 + [smem] * 2,
        out_specs=(vmem,) * 3,
        scratch_shapes=[
            like(query),
            like(incoming_key),
            like(new_value),
            like(key_cache),
            like(value_cache),
            like(out_weight),
            like(residual),
            like(pg),
            like(fg),
            like(vocab_weight),
            pltpu.VMEM(query.shape, F32),
            pltpu.VMEM((t_n, rows, model), F32),
            pltpu.VMEM((t_n - 1, rows, model), F32),
            pltpu.VMEM((t_n, rows, model), F32),
            pltpu.VMEM((slot_dev, fold), F32),
            pltpu.VMEM((t_n, slot_dev, fold), BF16),
            pltpu.VMEM((slot_dev, model), F32),
            pltpu.VMEM((chunks, dp_n, slot_dev, model // chunks), BF16),
            pltpu.VMEM((vloc, slots), F32),
            pltpu.VMEM((dp_n, 8, slots), jnp.int32),
            pltpu.VMEM((dp_n, 8, slots), F32),
            pltpu.VMEM((t_n, 8, slots), F32),
            dma((11,)),
            dma((tiles,)),
            dma((t_n - 1,)),
            dma((t_n - 1,)),
            dma((t_n - 1,)),
            dma((t_n - 1,)),
            dma((chunks, dp_n - 1)),
            dma((chunks, dp_n - 1)),
            dma((dp_n - 1,)),
            dma((dp_n - 1,)),
            dma((dp_n - 1,)),
            dma((dp_n - 1,)),
            dma((t_n - 1,)),
            dma((t_n - 1,)),
        ],
        compiler_params=pltpu.CompilerParams(
            collective_id=0, has_side_effects=True, vmem_limit_bytes=62 * 1024 * 1024
        ),
    )(
        query,
        incoming_key,
        new_value,
        key_cache,
        value_cache,
        cache_len,
        out_weight,
        residual,
        pg,
        fg,
        vocab_weight,
        sampled,
        stop_flag,
    )
    share = model // t_n
    new_residual = lax.dynamic_slice_in_dim(mixed, lax.axis_index("tensor") * share, share, 1)
    begin = lax.axis_index("dp") * slot_dev
    token_logprob = lax.dynamic_slice(logs, (0, begin), (1, slot_dev))[0]
    insert_rank = lax.dynamic_slice(ranks, (0, begin), (1, slot_dev))[0]
    return (new_residual, token_logprob, insert_rank, ranks[1, 0])


def solution(mesh):
    in_specs = (
        P("dp", "tensor"),
        P("dp", "tensor"),
        P("dp", "tensor"),
        P("dp", None, "tensor"),
        P("dp", None, "tensor"),
        P("dp"),
        P("tensor", None),
        P("dp", None),
        P(),
        P(),
        P(("dp", "tensor"), None),
        P("dp"),
        P("dp"),
    )
    out_specs = (P("dp", "tensor"), P("dp"), P("dp"), P())
    return jax.shard_map(
        functools.partial(on_device, mesh.shape["dp"], mesh.shape["tensor"]),
        mesh=mesh,
        in_specs=in_specs,
        out_specs=out_specs,
        check_vma=False,
    )
```

```python
import functools

import jax
import jax.numpy as jnp
from jax import lax
from jax.experimental import pallas as pl
from jax.experimental.pallas import tpu as pltpu
from jax.sharding import PartitionSpec as P

HEAD_DIM = 128
LANES = 128
MESH = pl.DeviceIdType.MESH
F32 = jnp.float32
BF16 = jnp.bfloat16
NT = (((1,), (1,)), ((), ()))


def chunk_count(model):
    for count in (3, 2):
        if model % (count * LANES) == 0:
            return count
    return 1


def kernel(
    dp_n,
    t_n,
    tiles,
    q_h,
    ik_h,
    nv_h,
    kc_h,
    vc_h,
    len_s,
    ow_h,
    res_h,
    pg_h,
    fg_h,
    w_h,
    samp_s,
    stop_s,
    nr_o,
    f_o,
    i_o,
    q,
    ik,
    nv,
    kc,
    vc,
    ow,
    res,
    pg,
    fg,
    w,
    attn,
    pfold,
    psend,
    precv,
    psum,
    resf,
    zfold,
    zbuf,
    nrf,
    hbuf,
    acc,
    ibuf,
    dstat,
    zstat,
    lsem,
    wsem,
    ps,
    pr,
    zs,
    zr,
    hs,
    hr,
    isn,
    irc,
    ds,
    dr,
    es,
    er,
):
    d = lax.axis_index("dp")
    t = lax.axis_index("tensor")
    slot_dev, model = res.shape
    positions = kc.shape[1]
    heads = q.shape[1] // HEAD_DIM
    kv = ik.shape[1] // HEAD_DIM
    group = heads // kv
    rows = slot_dev // t_n
    chunks = hbuf.shape[0]
    width = model // chunks
    slots = dp_n * slot_dev
    fold = zbuf.shape[2]
    chips = dp_n // 2
    half = slot_dev // 2
    vloc = w.shape[0]
    tile = vloc // tiles

    def at_dp(peer):
        return {"dp": peer, "tensor": t}

    def at_t(peer):
        return {"dp": d, "tensor": peer}

    barrier = pltpu.get_barrier_semaphore()
    for k in range(1, dp_n):
        pl.semaphore_signal(
            barrier, inc=1, device_id=at_dp((d + k) % dp_n), device_id_type=MESH
        )
    for k in range(1, t_n):
        pl.semaphore_signal(
            barrier, inc=1, device_id=at_t((t + k) % t_n), device_id_type=MESH
        )

    def local(src, dst, i):
        copy = pltpu.make_async_copy(src, dst, lsem.at[i])
        copy.start()
        return copy

    def remote(src, dst, s, r, dev):
        return pltpu.make_async_remote_copy(
            src_ref=src, dst_ref=dst, send_sem=s, recv_sem=r, device_id=dev, device_id_type=MESH
        )

    first = pl.ds(0, half)
    second = pl.ds(half, half)
    c_q = local(q_h, q, 0)
    c_ik = local(ik_h, ik, 1)
    c_k = [local(kc_h.at[first], kc.at[first], 2)]
    c_nv = local(nv_h, nv, 3)
    c_v = [local(vc_h.at[first], vc.at[first], 4)]
    c_k.append(local(kc_h.at[second], kc.at[second], 5))
    c_v.append(local(vc_h.at[second], vc.at[second], 6))
    c_ow = local(ow_h, ow, 7)
    c_res = local(res_h, res, 8)
    c_pg = local(pg_h, pg, 9)
    c_fg = local(fg_h, fg, 10)
    w_copies = [
        pltpu.make_async_copy(
            w_h.at[pl.ds(i * tile, tile)], w.at[pl.ds(i * tile, tile)], wsem.at[i]
        )
        for i in range(tiles)
    ]
    pending = list(w_copies)

    def issue(count):
        for _ in range(min(count, len(pending))):
            pending.pop(0).start()

    lane = lax.broadcasted_iota(jnp.int32, (8, slots), 1)
    sub = lax.broadcasted_iota(jnp.int32, (8, slots), 0)
    info = jnp.zeros((8, slots), jnp.int32)
    for i in range(slot_dev):
        freed = jnp.where(stop_s[i] == 1, 1, 0)
        info = jnp.where(lane == d * slot_dev + i, jnp.where(sub == 0, samp_s[i], freed), info)
    ibuf[d] = info

    pl.semaphore_wait(barrier, dp_n - 1 + t_n - 1)
    sent = []
    i_copies = []
    for k in range(1, dp_n):
        copy = remote(
            ibuf.at[d], ibuf.at[d], isn.at[k - 1], irc.at[k - 1], at_dp((d + k) % dp_n)
        )
        copy.start()
        i_copies.append(copy)
    sent += i_copies

    head_mask = lax.broadcasted_iota(
        jnp.int32, (heads, heads * HEAD_DIM), 1
    ) // HEAD_DIM == lax.broadcasted_iota(jnp.int32, (heads, heads * HEAD_DIM), 0)
    pos = lax.broadcasted_iota(jnp.int32, (heads, positions), 1)
    c_q.wait()
    c_ik.wait()
    qf = q[...].astype(F32)
    ikf = ik[...].astype(F32)
    for part in range(2):
        numbers = range(part * half, part * half + half)
        c_k[part].wait()
        issue(1)
        scores = []
        for b in numbers:
            x = jnp.where(head_mask, jnp.broadcast_to(qf[b : b + 1, :], head_mask.shape), 0.0)
            blocks = []
            for g in range(kv):
                block = x[:, g * group * HEAD_DIM : (g * group + 1) * HEAD_DIM]
                for j in range(g * group + 1, (g + 1) * group):
                    block = block + x[:, j * HEAD_DIM : (j + 1) * HEAD_DIM]
                blocks.append(block)
            spread = jnp.concatenate(blocks, axis=1)
            score = lax.dot_general(
                spread.astype(BF16), kc[b], NT, preferred_element_type=F32
            ) / 12.0
            own = jnp.sum(spread * ikf[b : b + 1, :], axis=1, keepdims=True) / 12.0
            scores.append((score, own))
        weights = []
        for b, (score, own) in zip(numbers, scores):
            valid = pos < len_s[b]
            score = jnp.where(valid, score, -1e30)
            top = jnp.maximum(jnp.max(score, axis=1, keepdims=True), own)
            expo = jnp.where(valid, jnp.exp(score - top), 0.0)
            own_exp = jnp.exp(own - top)
            total = jnp.sum(expo, axis=1, keepdims=True) + own_exp
            weights.append(((expo / total).astype(BF16), (own_exp / total).astype(BF16).astype(F32)))
        if part == 0:
            c_nv.wait()
            nvf = nv[...].astype(F32)
        c_v[part].wait()
        issue(1)
        for b, (weight, own) in zip(numbers, weights):
            mix = jnp.dot(weight, vc[b], preferred_element_type=F32) + own * nvf[b : b + 1, :]
            for h in range(heads):
                g = h // group
                attn[b : b + 1, h * HEAD_DIM : (h + 1) * HEAD_DIM] = mix[
                    h : h + 1, g * HEAD_DIM : (g + 1) * HEAD_DIM
                ]

    issue(1)
    c_res.wait()
    res_all = res[...].astype(F32)
    for s in range(t_n):
        resf[s] = res_all[s * rows : (s + 1) * rows, :]
    attn_b = attn[...].astype(BF16)
    c_ow.wait()
    issue(len(pending))
    padded = t_n * fold != model
    if padded:
        pfold[...] = jnp.zeros_like(pfold)
        zfold[...] = jnp.zeros_like(zfold)
    sizes = [min(fold, model - f * fold) for f in range(t_n)]
    for f in range(t_n):
        if sizes[f] > 0:
            partial = jnp.dot(
                attn_b, ow[:, f * fold : f * fold + sizes[f]], preferred_element_type=F32
            )
            for s in range(t_n):
                pfold[s, f * rows : (f + 1) * rows, 0 : sizes[f]] = partial[
                    s * rows : (s + 1) * rows, :
                ]
    psend[...] = pfold[...].astype(BF16)
    p_copies = []
    for k in range(1, t_n):
        peer = (t + k) % t_n
        copy = remote(psend.at[peer], precv.at[k - 1], ps.at[k - 1], pr.at[k - 1], at_t(peer))
        copy.start()
        p_copies.append(copy)
    sent += p_copies
    c_pg.wait()
    c_fg.wait()
    folded = pfold[t]
    for k in range(1, t_n):
        p_copies[k - 1].wait_recv()
        folded = folded + precv[k - 1].astype(F32)
    for f in range(t_n):
        if sizes[f] > 0:
            psum[:, f * fold : f * fold + sizes[f]] = folded[
                f * rows : (f + 1) * rows, 0 : sizes[f]
            ]
    proj = psum[...]
    post_gain = pg[...].reshape(1, model)
    post = proj * lax.rsqrt(jnp.mean(proj * proj, axis=1, keepdims=True) + 1e-06) * post_gain
    mixed = (resf[t] + post).astype(BF16).astype(F32)
    for s in range(t_n):
        size = min(fold, model - s * fold)
        if size > 0:
            zfold[s * rows : (s + 1) * rows, 0:size] = mixed[:, s * fold : s * fold + size]
    zbuf[t] = zfold[...].astype(BF16)
    z_copies = []
    for k in range(1, t_n):
        copy = remote(
            zbuf.at[t], zbuf.at[t], zs.at[k - 1], zr.at[k - 1], at_t((t + k) % t_n)
        )
        copy.start()
        z_copies.append(copy)
    sent += z_copies
    for copy in z_copies:
        copy.wait_recv()
    for s in range(t_n):
        piece = zbuf[s].astype(F32)
        for f in range(t_n):
            size = min(fold, model - f * fold)
            if size > 0:
                nrf[s * rows : (s + 1) * rows, f * fold : f * fold + size] = piece[
                    f * rows : (f + 1) * rows, 0:size
                ]
    mixed = nrf[...]
    final_gain = fg[...].reshape(1, model)
    hidden = (
        mixed * lax.rsqrt(jnp.mean(mixed * mixed, axis=1, keepdims=True) + 1e-06) * final_gain
    ).astype(BF16)

    sibling = d + 1 - 2 * (d % 2)
    direct = {}
    for c in range(chunks):
        hbuf[c, d] = hidden[:, c * width : (c + 1) * width]
        here = hbuf.at[c, d]
        for k in range(1, chips):
            direct[c, k] = remote(
                here, here, hs.at[c, k], hr.at[c, k], at_dp((d + 2 * k) % dp_n)
            )
            direct[c, k].start()
        direct[c, 0] = remote(here, here, hs.at[c, 0], hr.at[c, 0], at_dp(sibling))
        direct[c, 0].start()
    sent += list(direct.values())
    passed = {}

    def pass_on(c):
        for k in range(1, chips):
            direct[c, k].wait_recv()
            there = hbuf.at[c, (d + dp_n - 2 * k) % dp_n]
            j = chips - 1 + k
            passed[c, k] = remote(there, there, hs.at[c, j], hr.at[c, j], at_dp(sibling))
            passed[c, k].start()
            sent.append(passed[c, k])

    share = model // t_n
    mine = nrf[:, 0:share]
    for s in range(1, t_n):
        mine = jnp.where(t == s, nrf[:, s * share : (s + 1) * share], mine)
    nr_o[...] = mine.astype(BF16)

    def own_slots(row):
        kept = row[:, 0:slot_dev]
        for j in range(1, dp_n):
            kept = jnp.where(d == j, row[:, j * slot_dev : (j + 1) * slot_dev], kept)
        return kept

    for copy in i_copies:
        copy.wait_recv()
    info = ibuf[0]
    for j in range(1, dp_n):
        info = info + ibuf[j]
    flags = info[1:2, :]
    order = lax.broadcasted_iota(jnp.int32, (slots, slots), 0) < lax.broadcasted_iota(
        jnp.int32, (slots, slots), 1
    )
    flags8 = jnp.broadcast_to(flags, (8, slots)).astype(F32)
    before = jnp.dot(
        flags8.astype(BF16),
        jnp.where(order, 1.0, 0.0).astype(BF16),
        preferred_element_type=F32,
    )
    rank = jnp.where(flags8 > 0.5, before, -1.0)
    count = jnp.sum(flags8, axis=1, keepdims=True)
    i_o[...] = own_slots(jnp.where(sub == 0, rank, count)).astype(jnp.int32)
    start = (d * t_n + t) * vloc
    local_ids = info[0:1, :] - start

    pass_on(0)
    top = None
    for c in range(chunks):
        direct[c, 0].wait_recv()
        for k in range(1, chips):
            passed[c, k].wait_recv()
        state = hbuf[c].reshape(slots, width)
        for i in range(tiles):
            if c == 0:
                w_copies[i].wait()
            if c + 1 < chunks and i == tiles // 2:
                pass_on(c + 1)
            part = lax.dot_general(
                w[i * tile : (i + 1) * tile, c * width : (c + 1) * width],
                state,
                NT,
                preferred_element_type=F32,
            )
            if c > 0:
                part = part + acc[i * tile : (i + 1) * tile, :]
            if c + 1 < chunks:
                acc[i * tile : (i + 1) * tile, :] = part
                continue
            index = lax.broadcasted_iota(jnp.int32, (tile, slots), 0) + i * tile
            hit = jnp.sum(jnp.where(index == local_ids, part, 0.0), axis=0, keepdims=True)
            peak = jnp.max(part, axis=0, keepdims=True)
            if top is None:
                top = peak
                total = jnp.sum(jnp.exp(part - top), axis=0, keepdims=True)
                picked = hit
            else:
                larger = jnp.maximum(top, peak)
                total = total * jnp.exp(top - larger) + jnp.sum(
                    jnp.exp(part - larger), axis=0, keepdims=True
                )
                top = larger
                picked = picked + hit

    def pack(top, total, picked):
        return jnp.where(sub == 0, top, jnp.where(sub == 1, total, picked))

    def merge(parts):
        top = parts[0][0:1, :]
        for part in parts[1:]:
            top = jnp.maximum(top, part[0:1, :])
        total = jnp.zeros_like(top)
        picked = jnp.zeros_like(top)
        for part in parts:
            total = total + part[1:2, :] * jnp.exp(part[0:1, :] - top)
            picked = picked + part[2:3, :]
        return top, total, picked

    dstat[d] = pack(top, total, picked)
    copies = []
    for k in range(1, dp_n):
        copy = remote(dstat.at[d], dstat.at[d], ds.at[k - 1], dr.at[k - 1], at_dp((d + k) % dp_n))
        copy.start()
        copies.append(copy)
    for copy in copies:
        copy.wait_recv()
    sent += copies
    zstat[t] = pack(*merge([dstat[j] for j in range(dp_n)]))
    copies = []
    for k in range(1, t_n):
        copy = remote(zstat.at[t], zstat.at[t], es.at[k - 1], er.at[k - 1], at_t((t + k) % t_n))
        copy.start()
        copies.append(copy)
    for copy in copies:
        copy.wait_recv()
    sent += copies
    top, total, picked = merge([zstat[j] for j in range(t_n)])
    f_o[...] = own_slots(jnp.broadcast_to(picked - (jnp.log(total) + top), (8, slots)))
    for copy in sent:
        copy.wait_send()


def finish(mixed, logs, ranks, new_residual, token_logprob, insert_rank, total):
    new_residual[...] = mixed[...]
    token_logprob[...] = logs[0, :]
    insert_rank[...] = ranks[0, :]
    total[...] = ranks[1:2, 0:1]


def on_device(
    dp_n,
    t_n,
    query,
    incoming_key,
    new_value,
    key_cache,
    value_cache,
    cache_len,
    out_weight,
    residual,
    post_gain,
    final_gain,
    vocab_weight,
    sampled,
    stop_flag,
):
    slot_dev, model = residual.shape
    slots = slot_dev * dp_n
    rows = slot_dev // t_n
    fold = -(-model // (t_n * LANES)) * LANES
    chunks = chunk_count(model)
    vloc = vocab_weight.shape[0]
    tiles = max(1, vloc // 512)
    dma = pltpu.SemaphoreType.DMA
    anywhere = pl.BlockSpec(memory_space=pl.ANY)
    smem = pl.BlockSpec(memory_space=pltpu.SMEM)
    vmem = pl.BlockSpec(memory_space=pltpu.VMEM)

    def like(a):
        return pltpu.VMEM(a.shape, a.dtype)

    share = model // t_n
    mixed, logs, ranks = pl.pallas_call(
        functools.partial(kernel, dp_n, t_n, tiles),
        out_shape=(
            jax.ShapeDtypeStruct((slot_dev, share), BF16),
            jax.ShapeDtypeStruct((8, slot_dev), F32),
            jax.ShapeDtypeStruct((8, slot_dev), jnp.int32),
        ),
        in_specs=[anywhere] * 5 + [smem] + [anywhere] * 5 + [smem] * 2,
        out_specs=(vmem,) * 3,
        scratch_shapes=[
            like(query),
            like(incoming_key),
            like(new_value),
            like(key_cache),
            like(value_cache),
            like(out_weight),
            like(residual),
            like(post_gain),
            like(final_gain),
            like(vocab_weight),
            pltpu.VMEM(query.shape, F32),
            pltpu.VMEM((t_n, slot_dev, fold), F32),
            pltpu.VMEM((t_n, slot_dev, fold), BF16),
            pltpu.VMEM((t_n - 1, slot_dev, fold), BF16),
            pltpu.VMEM((rows, model), F32),
            pltpu.VMEM((t_n, rows, model), F32),
            pltpu.VMEM((slot_dev, fold), F32),
            pltpu.VMEM((t_n, slot_dev, fold), BF16),
            pltpu.VMEM((slot_dev, model), F32),
            pltpu.VMEM((chunks, dp_n, slot_dev, model // chunks), BF16),
            pltpu.VMEM((vloc, slots), F32),
            pltpu.VMEM((dp_n, 8, slots), jnp.int32),
            pltpu.VMEM((dp_n, 8, slots), F32),
            pltpu.VMEM((t_n, 8, slots), F32),
            dma((11,)),
            dma((tiles,)),
            dma((t_n - 1,)),
            dma((t_n - 1,)),
            dma((t_n - 1,)),
            dma((t_n - 1,)),
            dma((chunks, dp_n - 1)),
            dma((chunks, dp_n - 1)),
            dma((dp_n - 1,)),
            dma((dp_n - 1,)),
            dma((dp_n - 1,)),
            dma((dp_n - 1,)),
            dma((t_n - 1,)),
            dma((t_n - 1,)),
        ],
        compiler_params=pltpu.CompilerParams(
            collective_id=0, has_side_effects=True, vmem_limit_bytes=62 * 1024 * 1024
        ),
    )(
        query,
        incoming_key,
        new_value,
        key_cache,
        value_cache,
        cache_len,
        out_weight,
        residual,
        post_gain,
        final_gain,
        vocab_weight,
        sampled,
        stop_flag,
    )
    new_residual, token_logprob, insert_rank, total = pl.pallas_call(
        finish,
        out_shape=(
            jax.ShapeDtypeStruct((slot_dev, share), BF16),
            jax.ShapeDtypeStruct((slot_dev,), F32),
            jax.ShapeDtypeStruct((slot_dev,), jnp.int32),
            jax.ShapeDtypeStruct((1, 1), jnp.int32),
        ),
        in_specs=[vmem] * 3,
        out_specs=(vmem,) * 4,
    )(mixed, logs, ranks)
    return (new_residual, token_logprob, insert_rank, total.reshape(()))


def solution(mesh):
    in_specs = (
        P("dp", "tensor"),
        P("dp", "tensor"),
        P("dp", "tensor"),
        P("dp", None, "tensor"),
        P("dp", None, "tensor"),
        P("dp"),
        P("tensor", None),
        P("dp", None),
        P(),
        P(),
        P(("dp", "tensor"), None),
        P("dp"),
        P("dp"),
    )
    out_specs = (P("dp", "tensor"), P("dp"), P("dp"), P())
    return jax.shard_map(
        functools.partial(on_device, mesh.shape["dp"], mesh.shape["tensor"]),
        mesh=mesh,
        in_specs=in_specs,
        out_specs=out_specs,
        check_vma=False,
    )
```

```python
import functools

import jax
import jax.numpy as jnp
from jax import lax
from jax.experimental import pallas as pl
from jax.experimental.pallas import tpu as pltpu
from jax.sharding import PartitionSpec as P

HEAD_DIM = 128
LANES = 128
MESH = pl.DeviceIdType.MESH
F32 = jnp.float32
BF16 = jnp.bfloat16
NT = (((1,), (1,)), ((), ()))


def chunk_count(model):
    for count in (3, 2):
        if model % (count * LANES) == 0:
            return count
    return 1


def kernel(
    dp_n,
    t_n,
    tiles,
    q_h,
    ik_h,
    nv_h,
    kc_h,
    vc_h,
    len_s,
    ow_h,
    res_h,
    pg_h,
    fg_h,
    w_h,
    samp_s,
    stop_s,
    nr_o,
    f_o,
    i_o,
    q,
    ik,
    nv,
    kc,
    vc,
    ow,
    res,
    pg,
    fg,
    w,
    attn,
    pfold,
    psend,
    precv,
    psum,
    resf,
    zfold,
    zbuf,
    nrf,
    hbuf,
    acc,
    ibuf,
    dstat,
    zstat,
    lsem,
    wsem,
    ps,
    pr,
    zs,
    zr,
    hs,
    hr,
    isn,
    irc,
    ds,
    dr,
    es,
    er,
):
    d = lax.axis_index("dp")
    t = lax.axis_index("tensor")
    slot_dev, model = res.shape
    positions = kc.shape[1]
    heads = q.shape[1] // HEAD_DIM
    kv = ik.shape[1] // HEAD_DIM
    group = heads // kv
    rows = slot_dev // t_n
    chunks = hbuf.shape[0]
    width = model // chunks
    slots = dp_n * slot_dev
    fold = zbuf.shape[2]
    chips = dp_n // 2
    half = slot_dev // 2
    vloc = w.shape[0]
    tile = vloc // tiles

    def at_dp(peer):
        return {"dp": peer, "tensor": t}

    def at_t(peer):
        return {"dp": d, "tensor": peer}

    barrier = pltpu.get_barrier_semaphore()
    for k in range(1, dp_n):
        pl.semaphore_signal(
            barrier, inc=1, device_id=at_dp((d + k) % dp_n), device_id_type=MESH
        )
    for k in range(1, t_n):
        pl.semaphore_signal(
            barrier, inc=1, device_id=at_t((t + k) % t_n), device_id_type=MESH
        )

    def local(src, dst, i):
        copy = pltpu.make_async_copy(src, dst, lsem.at[i])
        copy.start()
        return copy

    def remote(src, dst, s, r, dev):
        return pltpu.make_async_remote_copy(
            src_ref=src, dst_ref=dst, send_sem=s, recv_sem=r, device_id=dev, device_id_type=MESH
        )

    first = pl.ds(0, half)
    second = pl.ds(half, half)
    c_q = local(q_h, q, 0)
    c_ik = local(ik_h, ik, 1)
    c_k = [local(kc_h.at[first], kc.at[first], 2)]
    c_nv = local(nv_h, nv, 3)
    c_v = [local(vc_h.at[first], vc.at[first], 4)]
    c_k.append(local(kc_h.at[second], kc.at[second], 5))
    c_v.append(local(vc_h.at[second], vc.at[second], 6))
    c_ow = local(ow_h, ow, 7)
    c_res = local(res_h, res, 8)
    c_pg = local(pg_h, pg, 9)
    c_fg = local(fg_h, fg, 10)
    w_copies = [
        pltpu.make_async_copy(
            w_h.at[pl.ds(i * tile, tile)], w.at[pl.ds(i * tile, tile)], wsem.at[i]
        )
        for i in range(tiles)
    ]
    pending = list(w_copies)

    def issue(count):
        for _ in range(min(count, len(pending))):
            pending.pop(0).start()

    lane = lax.broadcasted_iota(jnp.int32, (8, slots), 1)
    sub = lax.broadcasted_iota(jnp.int32, (8, slots), 0)
    info = jnp.zeros((8, slots), jnp.int32)
    for i in range(slot_dev):
        freed = jnp.where(stop_s[i] == 1, 1, 0)
        info = jnp.where(lane == d * slot_dev + i, jnp.where(sub == 0, samp_s[i], freed), info)
    ibuf[d] = info

    pl.semaphore_wait(barrier, dp_n - 1 + t_n - 1)
    sent = []
    i_copies = []
    for k in range(1, dp_n):
        copy = remote(
            ibuf.at[d], ibuf.at[d], isn.at[k - 1], irc.at[k - 1], at_dp((d + k) % dp_n)
        )
        copy.start()
        i_copies.append(copy)
    sent += i_copies

    head_mask = lax.broadcasted_iota(
        jnp.int32, (heads, heads * HEAD_DIM), 1
    ) // HEAD_DIM == lax.broadcasted_iota(jnp.int32, (heads, heads * HEAD_DIM), 0)
    pos = lax.broadcasted_iota(jnp.int32, (heads, positions), 1)
    c_q.wait()
    c_ik.wait()
    qf = q[...].astype(F32)
    ikf = ik[...].astype(F32)
    for part in range(2):
        numbers = range(part * half, part * half + half)
        c_k[part].wait()
        issue(1)
        scores = []
        for b in numbers:
            x = jnp.where(head_mask, jnp.broadcast_to(qf[b : b + 1, :], head_mask.shape), 0.0)
            blocks = []
            for g in range(kv):
                block = x[:, g * group * HEAD_DIM : (g * group + 1) * HEAD_DIM]
                for j in range(g * group + 1, (g + 1) * group):
                    block = block + x[:, j * HEAD_DIM : (j + 1) * HEAD_DIM]
                blocks.append(block)
            spread = jnp.concatenate(blocks, axis=1)
            score = lax.dot_general(
                spread.astype(BF16), kc[b], NT, preferred_element_type=F32
            ) / 12.0
            own = jnp.sum(spread * ikf[b : b + 1, :], axis=1, keepdims=True) / 12.0
            scores.append((score, own))
        weights = []
        for b, (score, own) in zip(numbers, scores):
            valid = pos < len_s[b]
            score = jnp.where(valid, score, -1e30)
            top = jnp.maximum(jnp.max(score, axis=1, keepdims=True), own)
            expo = jnp.where(valid, jnp.exp(score - top), 0.0)
            own_exp = jnp.exp(own - top)
            total = jnp.sum(expo, axis=1, keepdims=True) + own_exp
            weights.append(((expo / total).astype(BF16), (own_exp / total).astype(BF16).astype(F32)))
        if part == 0:
            c_nv.wait()
            nvf = nv[...].astype(F32)
        c_v[part].wait()
        issue(1)
        for b, (weight, own) in zip(numbers, weights):
            mix = jnp.dot(weight, vc[b], preferred_element_type=F32) + own * nvf[b : b + 1, :]
            for h in range(heads):
                g = h // group
                attn[b : b + 1, h * HEAD_DIM : (h + 1) * HEAD_DIM] = mix[
                    h : h + 1, g * HEAD_DIM : (g + 1) * HEAD_DIM
                ]

    issue(1)
    c_res.wait()
    res_all = res[...].astype(F32)
    for s in range(t_n):
        resf[s] = res_all[s * rows : (s + 1) * rows, :]
    attn_b = attn[...].astype(BF16)
    c_ow.wait()
    issue(len(pending))
    padded = t_n * fold != model
    if padded:
        pfold[...] = jnp.zeros_like(pfold)
        zfold[...] = jnp.zeros_like(zfold)
    sizes = [min(fold, model - f * fold) for f in range(t_n)]
    for f in range(t_n):
        if sizes[f] > 0:
            partial = jnp.dot(
                attn_b, ow[:, f * fold : f * fold + sizes[f]], preferred_element_type=F32
            )
            for s in range(t_n):
                pfold[s, f * rows : (f + 1) * rows, 0 : sizes[f]] = partial[
                    s * rows : (s + 1) * rows, :
                ]
    psend[...] = pfold[...].astype(BF16)
    p_copies = []
    for k in range(1, t_n):
        peer = (t + k) % t_n
        copy = remote(psend.at[peer], precv.at[k - 1], ps.at[k - 1], pr.at[k - 1], at_t(peer))
        copy.start()
        p_copies.append(copy)
    sent += p_copies
    c_pg.wait()
    c_fg.wait()
    folded = pfold[t]
    for k in range(1, t_n):
        p_copies[k - 1].wait_recv()
        folded = folded + precv[k - 1].astype(F32)
    for f in range(t_n):
        if sizes[f] > 0:
            psum[:, f * fold : f * fold + sizes[f]] = folded[
                f * rows : (f + 1) * rows, 0 : sizes[f]
            ]
    proj = psum[...]
    post_gain = pg[...].reshape(1, model)
    post = proj * lax.rsqrt(jnp.mean(proj * proj, axis=1, keepdims=True) + 1e-06) * post_gain
    mixed = (resf[t] + post).astype(BF16).astype(F32)
    for s in range(t_n):
        size = min(fold, model - s * fold)
        if size > 0:
            zfold[s * rows : (s + 1) * rows, 0:size] = mixed[:, s * fold : s * fold + size]
    zbuf[t] = zfold[...].astype(BF16)
    z_copies = []
    for k in range(1, t_n):
        copy = remote(
            zbuf.at[t], zbuf.at[t], zs.at[k - 1], zr.at[k - 1], at_t((t + k) % t_n)
        )
        copy.start()
        z_copies.append(copy)
    sent += z_copies
    for copy in z_copies:
        copy.wait_recv()
    for s in range(t_n):
        piece = zbuf[s].astype(F32)
        for f in range(t_n):
            size = min(fold, model - f * fold)
            if size > 0:
                nrf[s * rows : (s + 1) * rows, f * fold : f * fold + size] = piece[
                    f * rows : (f + 1) * rows, 0:size
                ]
    mixed = nrf[...]
    final_gain = fg[...].reshape(1, model)
    hidden = (
        mixed * lax.rsqrt(jnp.mean(mixed * mixed, axis=1, keepdims=True) + 1e-06) * final_gain
    ).astype(BF16)

    sibling = d + 1 - 2 * (d % 2)
    direct = {}
    for c in range(chunks):
        hbuf[c, d] = hidden[:, c * width : (c + 1) * width]
        here = hbuf.at[c, d]
        for k in range(1, chips):
            direct[c, k] = remote(
                here, here, hs.at[c, k], hr.at[c, k], at_dp((d + 2 * k) % dp_n)
            )
            direct[c, k].start()
        direct[c, 0] = remote(here, here, hs.at[c, 0], hr.at[c, 0], at_dp(sibling))
        direct[c, 0].start()
    sent += list(direct.values())
    passed = {}

    def pass_on(c):
        for k in range(1, chips):
            direct[c, k].wait_recv()
            there = hbuf.at[c, (d + dp_n - 2 * k) % dp_n]
            j = chips - 1 + k
            passed[c, k] = remote(there, there, hs.at[c, j], hr.at[c, j], at_dp(sibling))
            passed[c, k].start()
            sent.append(passed[c, k])

    share = model // t_n
    mine = nrf[:, 0:share]
    for s in range(1, t_n):
        mine = jnp.where(t == s, nrf[:, s * share : (s + 1) * share], mine)
    nr_o[...] = mine.astype(BF16)

    def own_slots(row):
        kept = row[:, 0:slot_dev]
        for j in range(1, dp_n):
            kept = jnp.where(d == j, row[:, j * slot_dev : (j + 1) * slot_dev], kept)
        return kept

    for copy in i_copies:
        copy.wait_recv()
    info = ibuf[0]
    for j in range(1, dp_n):
        info = info + ibuf[j]
    flags = info[1:2, :]
    order = lax.broadcasted_iota(jnp.int32, (slots, slots), 0) < lax.broadcasted_iota(
        jnp.int32, (slots, slots), 1
    )
    flags8 = jnp.broadcast_to(flags, (8, slots)).astype(F32)
    before = jnp.dot(
        flags8.astype(BF16),
        jnp.where(order, 1.0, 0.0).astype(BF16),
        preferred_element_type=F32,
    )
    rank = jnp.where(flags8 > 0.5, before, -1.0)
    count = jnp.sum(flags8, axis=1, keepdims=True)
    i_o[...] = own_slots(jnp.where(sub == 0, rank, count)).astype(jnp.int32)
    start = (d * t_n + t) * vloc
    local_ids = info[0:1, :] - start

    join = 2 if tiles % 2 == 0 else 1
    block = tile * join
    blocks = tiles // join
    pass_on(0)
    top = None
    for c in range(chunks):
        direct[c, 0].wait_recv()
        for k in range(1, chips):
            passed[c, k].wait_recv()
        state = hbuf[c].reshape(slots, width)
        for i in range(blocks):
            if c == 0:
                for copy in w_copies[i * join : (i + 1) * join]:
                    copy.wait()
            if c + 1 < chunks and i == blocks // 2:
                pass_on(c + 1)
            part = lax.dot_general(
                w[i * block : (i + 1) * block, c * width : (c + 1) * width],
                state,
                NT,
                preferred_element_type=F32,
            )
            if c > 0:
                part = part + acc[i * block : (i + 1) * block, :]
            if c + 1 < chunks:
                acc[i * block : (i + 1) * block, :] = part
                continue
            index = lax.broadcasted_iota(jnp.int32, (block, slots), 0) + i * block
            hit = jnp.sum(jnp.where(index == local_ids, part, 0.0), axis=0, keepdims=True)
            peak = jnp.max(part, axis=0, keepdims=True)
            if top is None:
                top = peak
                total = jnp.sum(jnp.exp(part - top), axis=0, keepdims=True)
                picked = hit
            else:
                larger = jnp.maximum(top, peak)
                total = total * jnp.exp(top - larger) + jnp.sum(
                    jnp.exp(part - larger), axis=0, keepdims=True
                )
                top = larger
                picked = picked + hit

    def pack(top, total, picked):
        return jnp.where(sub == 0, top, jnp.where(sub == 1, total, picked))

    def merge(parts):
        top = parts[0][0:1, :]
        for part in parts[1:]:
            top = jnp.maximum(top, part[0:1, :])
        total = jnp.zeros_like(top)
        picked = jnp.zeros_like(top)
        for part in parts:
            total = total + part[1:2, :] * jnp.exp(part[0:1, :] - top)
            picked = picked + part[2:3, :]
        return top, total, picked

    dstat[d] = pack(top, total, picked)
    copies = []
    for k in range(1, dp_n):
        copy = remote(dstat.at[d], dstat.at[d], ds.at[k - 1], dr.at[k - 1], at_dp((d + k) % dp_n))
        copy.start()
        copies.append(copy)
    for copy in copies:
        copy.wait_recv()
    sent += copies
    zstat[t] = pack(*merge([dstat[j] for j in range(dp_n)]))
    copies = []
    for k in range(1, t_n):
        copy = remote(zstat.at[t], zstat.at[t], es.at[k - 1], er.at[k - 1], at_t((t + k) % t_n))
        copy.start()
        copies.append(copy)
    for copy in copies:
        copy.wait_recv()
    sent += copies
    top, total, picked = merge([zstat[j] for j in range(t_n)])
    f_o[...] = own_slots(jnp.broadcast_to(picked - (jnp.log(total) + top), (8, slots)))
    for copy in sent:
        copy.wait_send()


def finish(mixed, logs, ranks, new_residual, token_logprob, insert_rank, total):
    new_residual[...] = mixed[...]
    token_logprob[...] = logs[0, :]
    insert_rank[...] = ranks[0, :]
    total[...] = ranks[1:2, 0:1]


def on_device(
    dp_n,
    t_n,
    query,
    incoming_key,
    new_value,
    key_cache,
    value_cache,
    cache_len,
    out_weight,
    residual,
    post_gain,
    final_gain,
    vocab_weight,
    sampled,
    stop_flag,
):
    slot_dev, model = residual.shape
    slots = slot_dev * dp_n
    rows = slot_dev // t_n
    fold = -(-model // (t_n * LANES)) * LANES
    chunks = chunk_count(model)
    vloc = vocab_weight.shape[0]
    tiles = max(1, vloc // 512)
    dma = pltpu.SemaphoreType.DMA
    anywhere = pl.BlockSpec(memory_space=pl.ANY)
    smem = pl.BlockSpec(memory_space=pltpu.SMEM)
    vmem = pl.BlockSpec(memory_space=pltpu.VMEM)

    def like(a):
        return pltpu.VMEM(a.shape, a.dtype)

    share = model // t_n
    mixed, logs, ranks = pl.pallas_call(
        functools.partial(kernel, dp_n, t_n, tiles),
        out_shape=(
            jax.ShapeDtypeStruct((slot_dev, share), BF16),
            jax.ShapeDtypeStruct((8, slot_dev), F32),
            jax.ShapeDtypeStruct((8, slot_dev), jnp.int32),
        ),
        in_specs=[anywhere] * 5 + [smem] + [anywhere] * 5 + [smem] * 2,
        out_specs=(vmem,) * 3,
        scratch_shapes=[
            like(query),
            like(incoming_key),
            like(new_value),
            like(key_cache),
            like(value_cache),
            like(out_weight),
            like(residual),
            like(post_gain),
            like(final_gain),
            like(vocab_weight),
            pltpu.VMEM(query.shape, F32),
            pltpu.VMEM((t_n, slot_dev, fold), F32),
            pltpu.VMEM((t_n, slot_dev, fold), BF16),
            pltpu.VMEM((t_n - 1, slot_dev, fold), BF16),
            pltpu.VMEM((rows, model), F32),
            pltpu.VMEM((t_n, rows, model), F32),
            pltpu.VMEM((slot_dev, fold), F32),
            pltpu.VMEM((t_n, slot_dev, fold), BF16),
            pltpu.VMEM((slot_dev, model), F32),
            pltpu.VMEM((chunks, dp_n, slot_dev, model // chunks), BF16),
            pltpu.VMEM((vloc, slots), F32),
            pltpu.VMEM((dp_n, 8, slots), jnp.int32),
            pltpu.VMEM((dp_n, 8, slots), F32),
            pltpu.VMEM((t_n, 8, slots), F32),
            dma((11,)),
            dma((tiles,)),
            dma((t_n - 1,)),
            dma((t_n - 1,)),
            dma((t_n - 1,)),
            dma((t_n - 1,)),
            dma((chunks, dp_n - 1)),
            dma((chunks, dp_n - 1)),
            dma((dp_n - 1,)),
            dma((dp_n - 1,)),
            dma((dp_n - 1,)),
            dma((dp_n - 1,)),
            dma((t_n - 1,)),
            dma((t_n - 1,)),
        ],
        compiler_params=pltpu.CompilerParams(
            collective_id=0, has_side_effects=True, vmem_limit_bytes=62 * 1024 * 1024
        ),
    )(
        query,
        incoming_key,
        new_value,
        key_cache,
        value_cache,
        cache_len,
        out_weight,
        residual,
        post_gain,
        final_gain,
        vocab_weight,
        sampled,
        stop_flag,
    )
    new_residual, token_logprob, insert_rank, total = pl.pallas_call(
        finish,
        out_shape=(
            jax.ShapeDtypeStruct((slot_dev, share), BF16),
            jax.ShapeDtypeStruct((slot_dev,), F32),
            jax.ShapeDtypeStruct((slot_dev,), jnp.int32),
            jax.ShapeDtypeStruct((1, 1), jnp.int32),
        ),
        in_specs=[vmem] * 3,
        out_specs=(vmem,) * 4,
    )(mixed, logs, ranks)
    return (new_residual, token_logprob, insert_rank, total.reshape(()))


def solution(mesh):
    in_specs = (
        P("dp", "tensor"),
        P("dp", "tensor"),
        P("dp", "tensor"),
        P("dp", None, "tensor"),
        P("dp", None, "tensor"),
        P("dp"),
        P("tensor", None),
        P("dp", None),
        P(),
        P(),
        P(("dp", "tensor"), None),
        P("dp"),
        P("dp"),
    )
    out_specs = (P("dp", "tensor"), P("dp"), P("dp"), P())
    return jax.shard_map(
        functools.partial(on_device, mesh.shape["dp"], mesh.shape["tensor"]),
        mesh=mesh,
        in_specs=in_specs,
        out_specs=out_specs,
        check_vma=False,
    )
```
